32 devices in a mesh: fsdp: 4 (over y, x), ctx: 8 (over z, core).
Axes of the slice: x: 2, y: 2, z: 4, core: 2. Of those that a mesh axis runs over, the one named last changes fastest.
Arguments:
- tokens: bfloat16 [8, 1024, 1024], P('fsdp', 'ctx'), may hold values from -6 to 6
- lengths: int32 [8], P('fsdp'), may hold values from 128 to 1024, as said below
- w_qkv: bfloat16 [1024, 3072], P('fsdp'), may hold values from -0.1875 to 0.1875
- b_qv: bfloat16 [2048], P('fsdp'), may hold values from -3 to 3
- w_out: bfloat16 [1024, 1024], P('fsdp'), may hold values from -3 to 3
- b_out: bfloat16 [1024], P('fsdp'), may hold values from -3 to 3
- gain_one: bfloat16 [1024], P('fsdp'), may hold values from 0.5 to 1.5
- shift_one: bfloat16 [1024], P('fsdp'), may hold values from -3 to 3
- w_up: bfloat16 [1024, 4096], P('fsdp'), may hold values from -0.1875 to 0.1875
- b_up: bfloat16 [4096], P('fsdp'), may hold values from -3 to 3
- w_down: bfloat16 [4096, 1024], P('fsdp'), may hold values from -0.09375 to 0.09375
- b_down: bfloat16 [1024], P('fsdp'), may hold values from -3 to 3
- gain_two: bfloat16 [1024], P('fsdp'), may hold values from 0.5 to 1.5
- shift_two: bfloat16 [1024], P('fsdp'), may hold values from -3 to 3
- cotangent: bfloat16 [8, 1024, 1024], P('fsdp', 'ctx'), may hold values from -6 to 6
Outputs:
- layer_out: bfloat16 [8, 1024, 1024], P('fsdp', 'ctx')
- grad_tokens: float32 [8, 1024, 1024], P('fsdp', 'ctx')
- grad_w_qkv: float32 [1024, 3072], P(('fsdp', 'ctx'))
- grad_b_qv: float32 [2048], P(('fsdp', 'ctx'))
- grad_w_out: float32 [1024, 1024], P(('fsdp', 'ctx'))
- grad_b_out: float32 [1024], P(('fsdp', 'ctx'))
- grad_gain_one: float32 [1024], P(('fsdp', 'ctx'))
- grad_shift_one: float32 [1024], P(('fsdp', 'ctx'))
- grad_w_up: float32 [1024, 4096], P(('fsdp', 'ctx'))
- grad_b_up: float32 [4096], P(('fsdp', 'ctx'))
- grad_w_down: float32 [4096, 1024], P(('fsdp', 'ctx'))
- grad_b_down: float32 [1024], P(('fsdp', 'ctx'))
- grad_gain_two: float32 [1024], P(('fsdp', 'ctx'))
- grad_shift_two: float32 [1024], P(('fsdp', 'ctx'))
The draws below stay inside these ranges and needn't reach their ends.
Inputs may be any that keep to these rules, and one draw needn't show every extreme that they name: `lengths`: among the 2 sequences on each index of fsdp, at least one has all 1024 positions valid; every sequence has at least its first 128 positions valid.
All inputs are finite; a program needn't handle non-finite values.
Results may differ from the reference program's by a relative error of at most 0.023.
Values may be sent and summed in bfloat16 or wider, within the bound.
A program may use at most 256 MiB of HBM per device.

```python
import jax
import jax.numpy as jnp
from jax import lax

D = 1024
HEAD = 64
FF = 4096
BLK = 128
SEQ_DEV = 2
SEQ_LEN = 1024
SEQS = 8


def draw_lengths(key, part):
    key = jax.random.fold_in(key, 11)
    first_key, second_key = jax.random.split(key)
    base_lengths = jax.random.randint(first_key, (SEQS,), BLK, SEQ_LEN + 1)
    group_count = SEQS // SEQ_DEV
    chosen = jax.random.randint(second_key, (group_count,), 0, SEQ_DEV)
    positions = jnp.arange(SEQS)
    full_row = positions % SEQ_DEV == jnp.repeat(chosen, SEQ_DEV)
    return jnp.where(full_row, SEQ_LEN, base_lengths).astype(jnp.int32)


def levels(stream_key, shape, shards, low, largest):
    loudness = 1.0
    for position, shards_of in shards:
        heights = jax.random.uniform(jax.random.fold_in(jax.random.fold_in(stream_key, 6), position), (shards_of,), jnp.float32, low / len(shards), largest / len(shards))
        loudness = loudness * jnp.repeat(jnp.exp(heights), shape[position] // shards_of).reshape((-1,) + (1,) * (len(shape) - 1 - position))
    return loudness


def centred(own_key, extent, width, most, cuts=(), dtype=jnp.bfloat16):
    entries = width * jax.random.normal(own_key, extent, jnp.float32)
    if cuts:
        entries = entries * levels(own_key, extent, cuts, -0.22, 0.18)
    return jnp.clip(entries, -most, most).astype(dtype)


def setup_inputs(seed: int = 0) -> dict:
    keys = jax.random.split(jax.random.key(seed), 16)
    tokens = centred(keys[0], (SEQS, SEQ_LEN, D), 1.0, 6.0, ((0, 4), (1, 8)))
    lengths = draw_lengths(jax.random.fold_in(keys[15], 71), 0)
    w_qkv = centred(keys[2], (D, 3 * D), D ** -0.5, 0.1875, ((0, 4),))
    b_qv = centred(keys[3], (2 * D,), 0.5, 3.0, ((0, 4),))
    w_out = centred(keys[4], (D, D), 4 ** -0.5, 3.0, ((0, 4),))
    b_out = centred(keys[5], (D,), 0.5, 3.0, ((0, 4),))
    gain_one = jnp.clip(1.0 + 0.1 * jax.random.normal(keys[6], (D,), jnp.float32), 0.5, 1.5).astype(jnp.bfloat16)
    shift_one = centred(keys[7], (D,), 0.5, 3.0, ((0, 4),))
    w_up = centred(keys[8], (D, FF), D ** -0.5, 0.1875, ((0, 4),))
    b_up = centred(keys[9], (FF,), 0.5, 3.0, ((0, 4),))
    w_down = centred(keys[10], (FF, D), FF ** -0.5, 0.09375, ((0, 4),))
    b_down = centred(keys[11], (D,), 0.5, 3.0, ((0, 4),))
    gain_two = jnp.clip(1.0 + 0.1 * jax.random.normal(keys[12], (D,), jnp.float32), 0.5, 1.5).astype(jnp.bfloat16)
    shift_two = centred(keys[13], (D,), 0.5, 3.0, ((0, 4),))
    cotangent = centred(keys[14], (SEQS, SEQ_LEN, D), 1.0, 6.0, ((0, 4), (1, 8)))
    return dict(tokens=tokens, lengths=lengths, w_qkv=w_qkv, b_qv=b_qv, w_out=w_out, b_out=b_out, gain_one=gain_one, shift_one=shift_one, w_up=w_up, b_up=b_up, w_down=w_down, b_down=b_down, gain_two=gain_two, shift_two=shift_two, cotangent=cotangent)


@jax.custom_vjp
def low(v):
    return lax.optimization_barrier(v.astype(jnp.bfloat16)).astype(jnp.float32)

@jax.custom_vjp
def low_back(v):
    return v

def low_keep(v):
    return (low(v), None)

def low_pass(kept, grad):
    return (grad,)

def back_keep(v):
    return (v, None)

def back_low(kept, grad):
    return (low(grad),)
low.defvjp(low_keep, low_pass)
low_back.defvjp(back_keep, back_low)
highest = lax.Precision.HIGHEST

def layer_norm(values, gain, shift):
    center = values - lax.optimization_barrier(jnp.mean(values, axis=-1, keepdims=True))
    spread = lax.optimization_barrier(jnp.mean(center * center, axis=-1, keepdims=True))
    return center * lax.rsqrt(spread + 1e-06) * gain + shift

def gelu_exact(inputs):
    return 0.5 * inputs * (1.0 + jax.scipy.special.erf(inputs * 0.7071067811865476))

def attend_block(query_block, keys_all, values_all, key_valid):
    scores = jnp.einsum('qhd,khd->hqk', query_block, keys_all, precision=highest) * HEAD ** (-0.5)
    scores = low_back(scores)
    scores = jnp.where(key_valid[None, None, :], scores, -1e+30)
    exponent = jnp.exp(scores - lax.optimization_barrier(jnp.max(scores, axis=-1, keepdims=True)))
    weights = low(exponent / lax.optimization_barrier(jnp.sum(exponent, axis=-1, keepdims=True)))
    return jnp.einsum('hqk,khd->qhd', weights, values_all, precision=highest)

def one_sequence(inputs, length, params):
    w_qkv, b_qv, w_out, b_out, gain_one, shift_one, w_up, b_up, w_down, b_down, gain_two, shift_two = params
    seq_len = inputs.shape[0]
    model_width = inputs.shape[1]
    head_count = model_width // HEAD
    mixed = jnp.dot(inputs, w_qkv, precision=highest)
    queries = low_back(low(mixed[:, :model_width] + b_qv[:model_width]))
    keys_all = low_back(low(mixed[:, model_width:2 * model_width]))
    values_all = low_back(low(mixed[:, 2 * model_width:] + b_qv[model_width:]))
    keys_heads = keys_all.reshape(seq_len, head_count, HEAD)
    values_heads = values_all.reshape(seq_len, head_count, HEAD)
    key_valid = jnp.arange(seq_len) < length
    block_rows = 4 * BLK
    query_blocks = queries.reshape(seq_len // block_rows, block_rows, head_count, HEAD)
    attended = lax.map(jax.checkpoint(lambda query_block: attend_block(query_block, keys_heads, values_heads, key_valid)), query_blocks)
    attended = low_back(low(attended.reshape(seq_len, model_width)))
    branch = low_back(jnp.dot(attended, w_out, precision=highest) + b_out)
    normed = layer_norm(inputs + branch, gain_one, shift_one)
    hidden = low_back(jnp.dot(low(normed), w_up, precision=highest) + b_up)
    activated = low(gelu_exact(hidden))
    outcome = low_back(jnp.dot(activated, w_down, precision=highest) + b_down)
    return layer_norm(normed + outcome, gain_two, shift_two)

def reference(tokens, lengths, w_qkv, b_qv, w_out, b_out, gain_one, shift_one, w_up, b_up, w_down, b_down, gain_two, shift_two, cotangent):
    params = tuple((weight_array.astype(jnp.float32) for weight_array in (w_qkv, b_qv, w_out, b_out, gain_one, shift_one, w_up, b_up, w_down, b_down, gain_two, shift_two)))

    def forward(inputs, *weights):
        return lax.map(lambda paired: one_sequence(paired[0], paired[1], weights), (inputs, lengths))
    outputs, pullback = jax.vjp(forward, tokens.astype(jnp.float32), *params)
    grads = pullback(cotangent.astype(jnp.float32))
    return (outputs.astype(jnp.bfloat16), grads[0], grads[1], grads[2], grads[3], grads[4], grads[5], grads[6], grads[7], grads[8], grads[9], grads[10], grads[11], grads[12])
```

```python
import jax
import jax.numpy as jnp
from jax import lax
from jax.experimental import pallas as pl
from jax.experimental.pallas import tpu as pltpu
from jax.sharding import PartitionSpec as P

HEAD = 64
GROUP = 2 * HEAD
VMEM_BYTES = 40 * 2**20


def shifted(value, axis, by):
    length = lax.axis_size(axis)
    return lax.ppermute(value, axis, [(i, (i + by) % length) for i in range(length)])


def norm_forward(values, gain, shift):
    center = values - jnp.mean(values, axis=-1, keepdims=True)
    inverse = lax.rsqrt(jnp.mean(center * center, axis=-1, keepdims=True) + 1e-06)
    normal_hat = center * inverse
    return (normal_hat * gain + shift, normal_hat, inverse)


def norm_backward(grad_out, normal_hat, inverse, gain):
    scaled = grad_out * gain
    return inverse * (
        scaled
        - jnp.mean(scaled, axis=-1, keepdims=True)
        - normal_hat * jnp.mean(scaled * normal_hat, axis=-1, keepdims=True)
    )


def gelu_exact(inputs):
    return 0.5 * inputs * (1.0 + jax.scipy.special.erf(inputs * 0.7071067811865476))


def gelu_slope(inputs):
    return (
        0.5 * (1.0 + jax.scipy.special.erf(inputs * 0.7071067811865476))
        + inputs * jnp.exp(-0.5 * inputs * inputs) * 0.3989422804014327
    )


def key_valid(lengths, offset, amount):
    positions = offset + jnp.arange(amount, dtype=jnp.int32)
    return (positions[None, :] < lengths[:, None])[:, None, None, :]


def block_terms(
    query_piece, d_att_piece, lse_piece, delta_piece, key_piece, value_piece, lengths, key_offset
):
    score_scale = HEAD ** (-0.5)
    scores = (
        jnp.einsum("sqhd,skhd->shqk", query_piece, key_piece, preferred_element_type=jnp.float32)
        * score_scale
    )
    scores = jnp.where(key_valid(lengths, key_offset, key_piece.shape[1]), scores, -1e30)
    probs = jnp.exp(scores - lse_piece[..., None])
    d_probs = jnp.einsum(
        "sqhd,skhd->shqk", d_att_piece, value_piece, preferred_element_type=jnp.float32
    )
    d_scores = (probs * (d_probs - delta_piece[..., None])).astype(jnp.bfloat16)
    query_term = (
        jnp.einsum("shqk,skhd->sqhd", d_scores, key_piece, preferred_element_type=jnp.float32)
        * score_scale
    )
    key_term = (
        jnp.einsum("shqk,sqhd->skhd", d_scores, query_piece, preferred_element_type=jnp.float32)
        * score_scale
    )
    value_term = jnp.einsum(
        "shqk,sqhd->skhd",
        probs.astype(jnp.bfloat16),
        d_att_piece,
        preferred_element_type=jnp.float32,
    )
    return (query_term, key_term, value_term)


def local(
    tokens,
    lengths,
    w_qkv,
    b_qv,
    w_out,
    b_out,
    gain_one,
    shift_one,
    w_up,
    b_up,
    w_down,
    b_down,
    gain_two,
    shift_two,
    cotangent,
):
    (
        wide_qkv,
        wide_bqv,
        wide_out,
        wide_bout,
        wide_gone,
        wide_sone,
        wide_up,
        wide_bup,
        wide_down,
        wide_bdown,
        wide_gtwo,
        wide_stwo,
    ) = (
        lax.all_gather(w_qkv, "fsdp", axis=0, tiled=True),
        lax.all_gather(b_qv, "fsdp", axis=0, tiled=True),
        lax.all_gather(w_out, "fsdp", axis=0, tiled=True),
        lax.all_gather(b_out, "fsdp", axis=0, tiled=True),
        lax.all_gather(gain_one, "fsdp", axis=0, tiled=True),
        lax.all_gather(shift_one, "fsdp", axis=0, tiled=True),
        lax.all_gather(w_up, "fsdp", axis=0, tiled=True),
        lax.all_gather(b_up, "fsdp", axis=0, tiled=True),
        lax.all_gather(w_down, "fsdp", axis=0, tiled=True),
        lax.all_gather(b_down, "fsdp", axis=0, tiled=True),
        lax.all_gather(gain_two, "fsdp", axis=0, tiled=True),
        lax.all_gather(shift_two, "fsdp", axis=0, tiled=True),
    )
    seq_count, blk_rows, model_width = tokens.shape
    head_count = model_width // HEAD
    row_count = seq_count * blk_rows
    score_scale = HEAD ** (-0.5)
    ctx_size = lax.axis_size("ctx")
    ctx_place = lax.axis_index("ctx")
    flat_rows = tokens.reshape(row_count, model_width)
    qv_bias = wide_bqv.astype(jnp.float32)
    mixed = jnp.dot(flat_rows, wide_qkv, preferred_element_type=jnp.float32)
    head_shape = (seq_count, blk_rows, head_count, HEAD)
    queries = (
        (mixed[:, :model_width] + qv_bias[:model_width]).astype(jnp.bfloat16).reshape(head_shape)
    )
    keys_low = mixed[:, model_width : 2 * model_width].astype(jnp.bfloat16).reshape(head_shape)
    values_low = (
        (mixed[:, 2 * model_width :] + qv_bias[model_width:])
        .astype(jnp.bfloat16)
        .reshape(head_shape)
    )
    stat_shape = (seq_count, head_count, blk_rows)
    running_max = jnp.full(stat_shape, -1e30, jnp.float32)
    key_piece = lax.all_gather(keys_low, "ctx", axis=1, tiled=True)
    value_piece = lax.all_gather(values_low, "ctx", axis=1, tiled=True)
    scores = (
        jnp.einsum("sqhd,skhd->shqk", queries, key_piece, preferred_element_type=jnp.float32)
        * score_scale
    )
    scores = jnp.where(key_valid(lengths, jnp.int32(0), key_piece.shape[1]), scores, -1e30)
    new_max = jnp.maximum(running_max, jnp.max(scores, axis=-1))
    weights = jnp.exp(scores - new_max[..., None])
    running_sum = jnp.sum(weights, axis=-1)
    running_acc = jnp.einsum(
        "shqk,skhd->shqd",
        weights.astype(jnp.bfloat16),
        value_piece,
        preferred_element_type=jnp.float32,
    )
    log_sums = new_max + jnp.log(running_sum)
    attended_heads = jnp.transpose(running_acc / running_sum[..., None], (0, 2, 1, 3))
    attended = attended_heads.reshape(row_count, model_width)
    attended_low = attended.astype(jnp.bfloat16)
    first_sum = (
        flat_rows.astype(jnp.float32)
        + jnp.dot(attended_low, wide_out, preferred_element_type=jnp.float32)
        + wide_bout.astype(jnp.float32)
    )
    gain_first = wide_gone.astype(jnp.float32)
    normed, hat_first, inv_first = norm_forward(
        first_sum, gain_first, wide_sone.astype(jnp.float32)
    )
    normed_low = normed.astype(jnp.bfloat16)
    hidden = jnp.dot(normed_low, wide_up, preferred_element_type=jnp.float32) + wide_bup.astype(
        jnp.float32
    )
    activated = gelu_exact(hidden).astype(jnp.bfloat16)
    second_sum = (
        normed
        + jnp.dot(activated, wide_down, preferred_element_type=jnp.float32)
        + wide_bdown.astype(jnp.float32)
    )
    gain_second = wide_gtwo.astype(jnp.float32)
    result, hat_second, inv_second = norm_forward(
        second_sum, gain_second, wide_stwo.astype(jnp.float32)
    )
    layer_out = result.astype(jnp.bfloat16).reshape(seq_count, blk_rows, model_width)
    grad_output = cotangent.reshape(row_count, model_width).astype(jnp.float32)
    grad_gtwo = jnp.sum(grad_output * hat_second, axis=0)
    grad_stwo = jnp.sum(grad_output, axis=0)
    d_second = norm_backward(grad_output, hat_second, inv_second, gain_second)
    d_out_low = d_second.astype(jnp.bfloat16)
    grad_wdown = jnp.einsum("ra,rb->ab", activated, d_out_low, preferred_element_type=jnp.float32)
    grad_bdown = jnp.sum(d_out_low, axis=0, dtype=jnp.float32)
    d_activated = jnp.einsum("rb,ab->ra", d_out_low, wide_down, preferred_element_type=jnp.float32)
    d_hidden = (d_activated * gelu_slope(hidden)).astype(jnp.bfloat16)
    grad_wup = jnp.einsum("ra,rb->ab", normed_low, d_hidden, preferred_element_type=jnp.float32)
    grad_bup = jnp.sum(d_hidden, axis=0, dtype=jnp.float32)
    d_normed = d_second + jnp.einsum(
        "rf,df->rd", d_hidden, wide_up, preferred_element_type=jnp.float32
    )
    grad_gone = jnp.sum(d_normed * hat_first, axis=0)
    grad_sone = jnp.sum(d_normed, axis=0)
    d_first = norm_backward(d_normed, hat_first, inv_first, gain_first)
    d_branch = d_first.astype(jnp.bfloat16)
    grad_wout = jnp.einsum("ra,rb->ab", attended_low, d_branch, preferred_element_type=jnp.float32)
    grad_bout = jnp.sum(d_branch, axis=0, dtype=jnp.float32)
    d_attended = jnp.einsum(
        "rb,ab->ra", d_branch, wide_out, preferred_element_type=jnp.float32
    ).astype(jnp.bfloat16)
    d_att_heads = d_attended.reshape(head_shape)
    delta_rows = jnp.einsum("sqhd,sqhd->shq", d_att_heads.astype(jnp.float32), attended_heads)
    zero_heads = jnp.zeros(head_shape, jnp.float32)

    def cycle_turn(turn_index, state_in):
        key_piece, value_piece, grad_keys, grad_values, grad_queries = state_in
        source = (ctx_place - turn_index) % ctx_size
        query_term, key_term, value_term = block_terms(
            queries,
            d_att_heads,
            log_sums,
            delta_rows,
            key_piece,
            value_piece,
            lengths,
            source * blk_rows,
        )
        key_piece, value_piece = shifted((key_piece, value_piece), "ctx", 1)
        grad_keys, grad_values = (
            shifted((grad_keys + key_term).astype(jnp.bfloat16), "ctx", 1).astype(jnp.float32),
            shifted((grad_values + value_term).astype(jnp.bfloat16), "ctx", 1).astype(jnp.float32),
        )
        return (key_piece, value_piece, grad_keys, grad_values, grad_queries + query_term)

    cycle_end = lax.fori_loop(
        0, ctx_size, cycle_turn, (keys_low, values_low, zero_heads, zero_heads, zero_heads)
    )
    grad_keys, grad_values, grad_queries = (cycle_end[2], cycle_end[3], cycle_end[4])
    d_mixed = jnp.concatenate(
        [
            grad_queries.reshape(row_count, model_width),
            grad_keys.reshape(row_count, model_width),
            grad_values.reshape(row_count, model_width),
        ],
        axis=1,
    ).astype(jnp.bfloat16)
    grad_wqkv = jnp.einsum("ra,rb->ab", flat_rows, d_mixed, preferred_element_type=jnp.float32)
    grad_bqv = jnp.concatenate(
        [
            jnp.sum(d_mixed[:, :model_width], axis=0, dtype=jnp.float32),
            jnp.sum(d_mixed[:, 2 * model_width :], axis=0, dtype=jnp.float32),
        ]
    )
    grad_tokens = d_first + jnp.einsum(
        "rc,dc->rd", d_mixed, wide_qkv, preferred_element_type=jnp.float32
    )
    grad_tokens = grad_tokens.reshape(seq_count, blk_rows, model_width)
    all_grads = (
        grad_wqkv,
        grad_bqv,
        grad_wout,
        grad_bout,
        grad_gone,
        grad_sone,
        grad_wup,
        grad_bup,
        grad_wdown,
        grad_bdown,
        grad_gtwo,
        grad_stwo,
    )
    partial_shares = (
        lax.psum_scatter(
            all_grads[0].astype(jnp.bfloat16), "fsdp", scatter_dimension=0, tiled=True
        ).astype(jnp.float32),
        lax.psum_scatter(
            all_grads[1].astype(jnp.bfloat16), "fsdp", scatter_dimension=0, tiled=True
        ).astype(jnp.float32),
        lax.psum_scatter(
            all_grads[2].astype(jnp.bfloat16), "fsdp", scatter_dimension=0, tiled=True
        ).astype(jnp.float32),
        lax.psum_scatter(
            all_grads[3].astype(jnp.bfloat16), "fsdp", scatter_dimension=0, tiled=True
        ).astype(jnp.float32),
        lax.psum_scatter(
            all_grads[4].astype(jnp.bfloat16), "fsdp", scatter_dimension=0, tiled=True
        ).astype(jnp.float32),
        lax.psum_scatter(
            all_grads[5].astype(jnp.bfloat16), "fsdp", scatter_dimension=0, tiled=True
        ).astype(jnp.float32),
        lax.psum_scatter(
            all_grads[6].astype(jnp.bfloat16), "fsdp", scatter_dimension=0, tiled=True
        ).astype(jnp.float32),
        lax.psum_scatter(
            all_grads[7].astype(jnp.bfloat16), "fsdp", scatter_dimension=0, tiled=True
        ).astype(jnp.float32),
        lax.psum_scatter(
            all_grads[8].astype(jnp.bfloat16), "fsdp", scatter_dimension=0, tiled=True
        ).astype(jnp.float32),
        lax.psum_scatter(
            all_grads[9].astype(jnp.bfloat16), "fsdp", scatter_dimension=0, tiled=True
        ).astype(jnp.float32),
        lax.psum_scatter(
            all_grads[10].astype(jnp.bfloat16), "fsdp", scatter_dimension=0, tiled=True
        ).astype(jnp.float32),
        lax.psum_scatter(
            all_grads[11].astype(jnp.bfloat16), "fsdp", scatter_dimension=0, tiled=True
        ).astype(jnp.float32),
    )
    shares = (
        lax.psum_scatter(
            partial_shares[0].astype(jnp.bfloat16), "ctx", scatter_dimension=0, tiled=True
        ).astype(jnp.float32),
        lax.psum_scatter(
            partial_shares[1].astype(jnp.bfloat16), "ctx", scatter_dimension=0, tiled=True
        ).astype(jnp.float32),
        lax.psum_scatter(
            partial_shares[2].astype(jnp.bfloat16), "ctx", scatter_dimension=0, tiled=True
        ).astype(jnp.float32),
        lax.psum_scatter(
            partial_shares[3].astype(jnp.bfloat16), "ctx", scatter_dimension=0, tiled=True
        ).astype(jnp.float32),
        lax.psum_scatter(
            partial_shares[4].astype(jnp.bfloat16), "ctx", scatter_dimension=0, tiled=True
        ).astype(jnp.float32),
        lax.psum_scatter(
            partial_shares[5].astype(jnp.bfloat16), "ctx", scatter_dimension=0, tiled=True
        ).astype(jnp.float32),
        lax.psum_scatter(
            partial_shares[6].astype(jnp.bfloat16), "ctx", scatter_dimension=0, tiled=True
        ).astype(jnp.float32),
        lax.psum_scatter(
            partial_shares[7].astype(jnp.bfloat16), "ctx", scatter_dimension=0, tiled=True
        ).astype(jnp.float32),
        lax.psum_scatter(
            partial_shares[8].astype(jnp.bfloat16), "ctx", scatter_dimension=0, tiled=True
        ).astype(jnp.float32),
        lax.psum_scatter(
            partial_shares[9].astype(jnp.bfloat16), "ctx", scatter_dimension=0, tiled=True
        ).astype(jnp.float32),
        lax.psum_scatter(
            partial_shares[10].astype(jnp.bfloat16), "ctx", scatter_dimension=0, tiled=True
        ).astype(jnp.float32),
        lax.psum_scatter(
            partial_shares[11].astype(jnp.bfloat16), "ctx", scatter_dimension=0, tiled=True
        ).astype(jnp.float32),
    )
    return (
        layer_out,
        grad_tokens,
        shares[0],
        shares[1],
        shares[2],
        shares[3],
        shares[4],
        shares[5],
        shares[6],
        shares[7],
        shares[8],
        shares[9],
        shares[10],
        shares[11],
    )


def swap_core(value):
    length = lax.axis_size("ctx")
    return lax.ppermute(value, "ctx", [(i, i ^ 1) for i in range(length)])


def hop(value, bit):
    return lax.ppermute(value, "fsdp", [(i, i ^ bit) for i in range(4)])


def take(value, place, axis=0):
    return lax.dynamic_index_in_dim(value, place, axis, keepdims=False)


def gather_weight(shard):
    place, core = lax.axis_index("fsdp"), lax.axis_index("ctx") % 2
    rows = shard.shape[0]
    half, quarter = rows // 2, rows // 4
    own = lax.dynamic_slice_in_dim(shard, core * half, half, 0)
    from_x, from_y = hop(own, 1), hop(own, 2)
    far = jnp.concatenate([hop(from_x[:quarter], 2), hop(from_y[quarter:], 1)], axis=0)
    whole = jnp.zeros((4 * rows,) + shard.shape[1:], shard.dtype)
    whole = lax.dynamic_update_slice_in_dim(whole, shard, place * rows, 0)
    for bit, piece in ((1, from_x), (2, from_y), (3, far)):
        start = (place ^ bit) * rows
        whole = lax.dynamic_update_slice_in_dim(whole, piece, start + core * half, 0)
        whole = lax.dynamic_update_slice_in_dim(
            whole, swap_core(piece), start + (1 - core) * half, 0
        )
    return whole


def reduce_weight(left, right):
    place, core = lax.axis_index("fsdp"), lax.axis_index("ctx") % 2
    ctx_size = lax.axis_size("ctx")
    rows, width = left.shape
    share = width // (4 * ctx_size)
    split = left.reshape(rows, width // (2 * share), 2, share)

    def product(which):
        part = take(split, which, 2).reshape(rows, width // 2)
        return jnp.einsum("ra,rb->ab", part, right, preferred_element_type=jnp.float32)

    given = swap_core(product(1 - core).astype(jnp.bfloat16))
    sums = (product(core) + given.astype(jnp.float32)).astype(jnp.bfloat16)
    sums = sums.reshape(4, width // 8, right.shape[1])
    half = width // 16
    far = take(sums, place ^ 3)
    pass_y, pass_x = hop(far[:half], 1), hop(far[half:], 2)
    for_x, for_y = take(sums, place ^ 1), take(sums, place ^ 2)
    got_x = hop(jnp.concatenate([for_x[:half], for_x[half:] + pass_x], axis=0), 1)
    got_y = hop(jnp.concatenate([for_y[:half] + pass_y, for_y[half:]], axis=0), 2)
    mine = (
        take(sums, place).astype(jnp.float32)
        + got_x.astype(jnp.float32)
        + got_y.astype(jnp.float32)
    ).astype(jnp.bfloat16)
    groups = [[2 * i + c for i in range(ctx_size // 2)] for c in range(2)]
    return lax.psum_scatter(
        mine, "ctx", scatter_dimension=0, tiled=True, axis_index_groups=groups
    ).astype(jnp.float32)


def exchange(value):
    return lax.all_to_all(value, "ctx", split_axis=0, concat_axis=0, tiled=True)


def dot_rows(left, right):
    return lax.dot_general(
        left, right, (((1,), (1,)), ((), ())), preferred_element_type=jnp.float32
    )


def head_probs(query, key, valid):
    scores = jnp.where(valid, dot_rows(query, key) * (HEAD ** (-0.5)), -1e30)
    weights = jnp.exp(scores - jnp.max(scores, axis=1, keepdims=True))
    return weights, jnp.sum(weights, axis=1, keepdims=True)


def merged(ref):
    value = ref[...]
    return value.reshape(value.shape[0] * value.shape[2], value.shape[3])


def attend_kernel(lengths_ref, query_ref, key_ref, value_ref, out_ref):
    query, key, value = merged(query_ref), merged(key_ref), merged(value_ref)
    rows, keys = query.shape[0], key.shape[0]
    valid = lax.broadcasted_iota(jnp.int32, (rows, keys), 1) < lengths_ref[pl.program_id(0)]
    lower = lax.broadcasted_iota(jnp.int32, (rows, GROUP), 1) < HEAD
    outs = []
    for head in range(2):
        picked = jnp.where(lower == (head == 0), query, jnp.zeros_like(query))
        weights, total = head_probs(picked, key, valid)
        acc = jnp.dot(weights.astype(jnp.bfloat16), value, preferred_element_type=jnp.float32)
        outs.append(acc / total)
    out = jnp.where(lower, outs[0], outs[1]).astype(jnp.bfloat16)
    out_ref[...] = out.reshape(out_ref.shape)


def attend_back_kernel(
    lengths_ref, query_ref, key_ref, value_ref, grad_ref, out_ref, key_acc, value_acc
):
    step = pl.program_id(1)
    query, key, value, grad = (
        merged(query_ref),
        merged(key_ref),
        merged(value_ref),
        merged(grad_ref),
    )
    rows, keys = query.shape[0], key.shape[0]
    blocks = query_ref.shape[0]
    valid = lax.broadcasted_iota(jnp.int32, (rows, keys), 1) < lengths_ref[pl.program_id(0)]
    lower = lax.broadcasted_iota(jnp.int32, (rows, GROUP), 1) < HEAD

    @pl.when(step == 0)
    def _():
        key_acc[...] = jnp.zeros_like(key_acc)
        value_acc[...] = jnp.zeros_like(value_acc)

    grads = []
    for head in range(2):
        mine = lower == (head == 0)
        picked = jnp.where(mine, query, jnp.zeros_like(query))
        picked_grad = jnp.where(mine, grad, jnp.zeros_like(grad))
        weights, total = head_probs(picked, key, valid)
        probs = weights / total
        d_probs = dot_rows(picked_grad, value)
        delta = jnp.sum(probs * d_probs, axis=1, keepdims=True)
        d_scores = (probs * (d_probs - delta)).astype(jnp.bfloat16)
        over_rows = (((0,), (0,)), ((), ()))
        value_acc[...] += lax.dot_general(
            probs.astype(jnp.bfloat16), picked_grad, over_rows, preferred_element_type=jnp.float32
        )
        key_acc[...] += lax.dot_general(
            d_scores, picked, over_rows, preferred_element_type=jnp.float32
        )
        grads.append(jnp.dot(d_scores, key, preferred_element_type=jnp.float32))
    d_query = jnp.where(lower, grads[0], grads[1]) * (HEAD ** (-0.5))
    out_ref[pl.ds(step * blocks, blocks), :, :, 0:GROUP] = d_query.astype(jnp.bfloat16).reshape(
        query_ref.shape
    )

    @pl.when(step == pl.num_programs(1) - 1)
    def _():
        shape = key_ref.shape
        d_key = (key_acc[...] * (HEAD ** (-0.5))).astype(jnp.bfloat16)
        out_ref[:, :, :, GROUP : 2 * GROUP] = d_key.reshape(shape)
        out_ref[:, :, :, 2 * GROUP : 3 * GROUP] = value_acc[...].astype(jnp.bfloat16).reshape(shape)


def attend_specs(parts, blk_rows, blocks):
    def query_part(s, i):
        return (i, s, 0, 0)

    def whole_part(which):
        return pl.BlockSpec((parts, 1, blk_rows, GROUP), lambda s, i: (0, s, 0, which))

    query_spec = pl.BlockSpec((blocks, 1, blk_rows, GROUP), query_part)
    return query_spec, whole_part(1), whole_part(2)


def attend(lengths, packed, blocks=2):
    parts, seq_count, blk_rows, _ = packed.shape
    query_spec, key_spec, value_spec = attend_specs(parts, blk_rows, blocks)
    return pl.pallas_call(
        attend_kernel,
        grid=(seq_count, parts // blocks),
        in_specs=[pl.BlockSpec(memory_space=pltpu.SMEM), query_spec, key_spec, value_spec],
        out_specs=query_spec,
        out_shape=jax.ShapeDtypeStruct((parts, seq_count, blk_rows, GROUP), jnp.bfloat16),
        compiler_params=pltpu.CompilerParams(vmem_limit_bytes=VMEM_BYTES),
        cost_estimate=pl.CostEstimate(
            flops=8 * GROUP * seq_count * (parts * blk_rows) ** 2,
            bytes_accessed=8 * seq_count * parts * blk_rows * GROUP,
            transcendentals=2 * seq_count * (parts * blk_rows) ** 2,
        ),
    )(lengths, packed, packed, packed)


def attend_back(lengths, packed, grad, blocks=2):
    parts, seq_count, blk_rows, width = packed.shape
    query_spec, key_spec, value_spec = attend_specs(parts, blk_rows, blocks)
    return pl.pallas_call(
        attend_back_kernel,
        grid=(seq_count, parts // blocks),
        in_specs=[
            pl.BlockSpec(memory_space=pltpu.SMEM),
            query_spec,
            key_spec,
            value_spec,
            query_spec,
        ],
        out_specs=pl.BlockSpec((parts, 1, blk_rows, width), lambda s, i: (0, s, 0, 0)),
        out_shape=jax.ShapeDtypeStruct(packed.shape, jnp.bfloat16),
        scratch_shapes=[pltpu.VMEM((parts * blk_rows, GROUP), jnp.float32)] * 2,
        compiler_params=pltpu.CompilerParams(vmem_limit_bytes=VMEM_BYTES),
        cost_estimate=pl.CostEstimate(
            flops=20 * GROUP * seq_count * (parts * blk_rows) ** 2,
            bytes_accessed=16 * seq_count * parts * blk_rows * GROUP,
            transcendentals=2 * seq_count * (parts * blk_rows) ** 2,
        ),
    )(lengths, packed, packed, packed, grad)


def local_heads(
    tokens,
    lengths,
    w_qkv,
    b_qv,
    w_out,
    b_out,
    gain_one,
    shift_one,
    w_up,
    b_up,
    w_down,
    b_down,
    gain_two,
    shift_two,
    cotangent,
):
    ctx_size = lax.axis_size("ctx")
    place, ctx_place = lax.axis_index("fsdp"), lax.axis_index("ctx")
    seq_count, blk_rows, model_width = tokens.shape
    row_count = seq_count * blk_rows
    wide_qkv = gather_weight(w_qkv)
    vectors = (b_qv, b_out, gain_one, shift_one, b_up, b_down, gain_two, shift_two)
    joined = lax.all_gather(jnp.concatenate(vectors), "fsdp", axis=0, tiled=False)
    wide, start = [], 0
    for vector in vectors:
        stop = start + vector.shape[0]
        wide.append(joined[:, start:stop].reshape(-1).astype(jnp.float32))
        start = stop
    qv_bias, out_bias, gain_first, shift_first, up_bias, down_bias, gain_second, shift_second = wide
    wide_out = gather_weight(w_out)
    wide_up = gather_weight(w_up)
    wide_down = gather_weight(w_down)
    flat_rows = tokens.reshape(row_count, model_width)
    mixed = jnp.dot(flat_rows, wide_qkv, preferred_element_type=jnp.float32)
    mixed_bias = jnp.concatenate(
        [qv_bias[:model_width], jnp.zeros((model_width,), jnp.float32), qv_bias[model_width:]]
    )
    mixed_low = (mixed + mixed_bias).astype(jnp.bfloat16)
    packed = jnp.transpose(
        mixed_low.reshape(seq_count, blk_rows, 3, ctx_size, GROUP), (3, 0, 1, 2, 4)
    ).reshape(ctx_size, seq_count, blk_rows, 3 * GROUP)
    packed = exchange(packed)
    attended_low = jnp.transpose(exchange(attend(lengths, packed)), (1, 2, 0, 3)).reshape(
        row_count, model_width
    )
    first_sum = (
        flat_rows.astype(jnp.float32)
        + jnp.dot(attended_low, wide_out, preferred_element_type=jnp.float32)
        + out_bias
    )
    normed, hat_first, inv_first = norm_forward(first_sum, gain_first, shift_first)
    normed_low = normed.astype(jnp.bfloat16)
    hidden = jnp.dot(normed_low, wide_up, preferred_element_type=jnp.float32) + up_bias
    activated = gelu_exact(hidden).astype(jnp.bfloat16)
    second_sum = (
        normed + jnp.dot(activated, wide_down, preferred_element_type=jnp.float32) + down_bias
    )
    result, hat_second, inv_second = norm_forward(second_sum, gain_second, shift_second)
    layer_out = result.astype(jnp.bfloat16).reshape(seq_count, blk_rows, model_width)
    grad_output = cotangent.reshape(row_count, model_width).astype(jnp.float32)
    grad_gtwo = jnp.sum(grad_output * hat_second, axis=0)
    grad_stwo = jnp.sum(grad_output, axis=0)
    d_second = norm_backward(grad_output, hat_second, inv_second, gain_second)
    d_out_low = d_second.astype(jnp.bfloat16)
    share_down = reduce_weight(activated, d_out_low)
    grad_bdown = jnp.sum(d_out_low, axis=0, dtype=jnp.float32)
    d_activated = jnp.einsum("rb,ab->ra", d_out_low, wide_down, preferred_element_type=jnp.float32)
    d_hidden = (d_activated * gelu_slope(hidden)).astype(jnp.bfloat16)
    share_up = reduce_weight(normed_low, d_hidden)
    grad_bup = jnp.sum(d_hidden, axis=0, dtype=jnp.float32)
    d_normed = d_second + jnp.einsum(
        "rf,df->rd", d_hidden, wide_up, preferred_element_type=jnp.float32
    )
    grad_gone = jnp.sum(d_normed * hat_first, axis=0)
    grad_sone = jnp.sum(d_normed, axis=0)
    d_first = norm_backward(d_normed, hat_first, inv_first, gain_first)
    d_branch = d_first.astype(jnp.bfloat16)
    share_out = reduce_weight(attended_low, d_branch)
    grad_bout = jnp.sum(d_branch, axis=0, dtype=jnp.float32)
    d_attended = jnp.einsum(
        "rb,ab->ra", d_branch, wide_out, preferred_element_type=jnp.float32
    ).astype(jnp.bfloat16)
    d_packed = jnp.transpose(
        d_attended.reshape(seq_count, blk_rows, ctx_size, GROUP), (2, 0, 1, 3)
    )
    d_parts = exchange(attend_back(lengths, packed, exchange(d_packed)))
    d_mixed = jnp.transpose(
        d_parts.reshape(ctx_size, seq_count, blk_rows, 3, GROUP), (1, 2, 3, 0, 4)
    ).reshape(row_count, 3 * model_width)
    share_qkv = reduce_weight(flat_rows, d_mixed)
    grad_bqv = jnp.concatenate(
        [
            jnp.sum(d_mixed[:, :model_width], axis=0, dtype=jnp.float32),
            jnp.sum(d_mixed[:, 2 * model_width :], axis=0, dtype=jnp.float32),
        ]
    )
    grad_tokens = d_first + jnp.einsum(
        "rc,dc->rd", d_mixed, wide_qkv, preferred_element_type=jnp.float32
    )
    grad_tokens = grad_tokens.reshape(seq_count, blk_rows, model_width)
    small = (
        grad_bqv,
        grad_bout,
        grad_gone,
        grad_sone,
        grad_bup,
        grad_bdown,
        grad_gtwo,
        grad_stwo,
    )
    device_count = 4 * ctx_size
    joined = jnp.concatenate([item.reshape(device_count, -1) for item in small], axis=1)
    joined = take(lax.psum(joined, ("fsdp", "ctx")), place * ctx_size + ctx_place)
    shares, start = [], 0
    for item in small:
        stop = start + item.shape[0] // device_count
        shares.append(joined[start:stop])
        start = stop
    return (
        layer_out,
        grad_tokens,
        share_qkv,
        shares[0],
        share_out,
        shares[1],
        shares[2],
        shares[3],
        share_up,
        shares[4],
        share_down,
        shares[5],
        shares[6],
        shares[7],
    )


def solution(mesh):
    by_heads = mesh.shape["fsdp"] == 4 and mesh.shape["ctx"] == 8
    return jax.shard_map(
        local_heads if by_heads else local,
        mesh=mesh,
        in_specs=(
            P("fsdp", "ctx", None),
            P("fsdp"),
            P("fsdp", None),
            P("fsdp"),
            P("fsdp", None),
            P("fsdp"),
            P("fsdp"),
            P("fsdp"),
            P("fsdp", None),
            P("fsdp"),
            P("fsdp", None),
            P("fsdp"),
            P("fsdp"),
            P("fsdp"),
            P("fsdp", "ctx", None),
        ),
        out_specs=(
            P("fsdp", "ctx", None),
            P("fsdp", "ctx", None),
            P(("fsdp", "ctx"), None),
            P(("fsdp", "ctx")),
            P(("fsdp", "ctx"), None),
            P(("fsdp", "ctx")),
            P(("fsdp", "ctx")),
            P(("fsdp", "ctx")),
            P(("fsdp", "ctx"), None),
            P(("fsdp", "ctx")),
            P(("fsdp", "ctx"), None),
            P(("fsdp", "ctx")),
            P(("fsdp", "ctx")),
            P(("fsdp", "ctx")),
        ),
        check_vma=False,
    )
```

```python
import jax
import jax.numpy as jnp
from jax import lax
from jax.experimental import pallas as pl
from jax.experimental.pallas import tpu as pltpu
from jax.sharding import PartitionSpec as P

HEAD = 64
GROUP = 2 * HEAD
VMEM_BYTES = 40 * 2**20


def shifted(value, axis, by):
    length = lax.axis_size(axis)
    return lax.ppermute(value, axis, [(i, (i + by) % length) for i in range(length)])


def norm_forward(values, gain, shift):
    center = values - jnp.mean(values, axis=-1, keepdims=True)
    inverse = lax.rsqrt(jnp.mean(center * center, axis=-1, keepdims=True) + 1e-06)
    normal_hat = center * inverse
    return (normal_hat * gain + shift, normal_hat, inverse)


def norm_backward(grad_out, normal_hat, inverse, gain):
    scaled = grad_out * gain
    return inverse * (
        scaled
        - jnp.mean(scaled, axis=-1, keepdims=True)
        - normal_hat * jnp.mean(scaled * normal_hat, axis=-1, keepdims=True)
    )


def gelu_exact(inputs):
    return 0.5 * inputs * (1.0 + jax.scipy.special.erf(inputs * 0.7071067811865476))


def gelu_slope(inputs):
    return (
        0.5 * (1.0 + jax.scipy.special.erf(inputs * 0.7071067811865476))
        + inputs * jnp.exp(-0.5 * inputs * inputs) * 0.3989422804014327
    )


def key_valid(lengths, offset, amount):
    positions = offset + jnp.arange(amount, dtype=jnp.int32)
    return (positions[None, :] < lengths[:, None])[:, None, None, :]


def block_terms(
    query_piece, d_att_piece, lse_piece, delta_piece, key_piece, value_piece, lengths, key_offset
):
    score_scale = HEAD ** (-0.5)
    scores = (
        jnp.einsum("sqhd,skhd->shqk", query_piece, key_piece, preferred_element_type=jnp.float32)
        * score_scale
    )
    scores = jnp.where(key_valid(lengths, key_offset, key_piece.shape[1]), scores, -1e30)
    probs = jnp.exp(scores - lse_piece[..., None])
    d_probs = jnp.einsum(
        "sqhd,skhd->shqk", d_att_piece, value_piece, preferred_element_type=jnp.float32
    )
    d_scores = (probs * (d_probs - delta_piece[..., None])).astype(jnp.bfloat16)
    query_term = (
        jnp.einsum("shqk,skhd->sqhd", d_scores, key_piece, preferred_element_type=jnp.float32)
        * score_scale
    )
    key_term = (
        jnp.einsum("shqk,sqhd->skhd", d_scores, query_piece, preferred_element_type=jnp.float32)
        * score_scale
    )
    value_term = jnp.einsum(
        "shqk,sqhd->skhd",
        probs.astype(jnp.bfloat16),
        d_att_piece,
        preferred_element_type=jnp.float32,
    )
    return (query_term, key_term, value_term)


def local(
    tokens,
    lengths,
    w_qkv,
    b_qv,
    w_out,
    b_out,
    gain_one,
    shift_one,
    w_up,
    b_up,
    w_down,
    b_down,
    gain_two,
    shift_two,
    cotangent,
):
    (
        wide_qkv,
        wide_bqv,
        wide_out,
        wide_bout,
        wide_gone,
        wide_sone,
        wide_up,
        wide_bup,
        wide_down,
        wide_bdown,
        wide_gtwo,
        wide_stwo,
    ) = (
        lax.all_gather(w_qkv, "fsdp", axis=0, tiled=True),
        lax.all_gather(b_qv, "fsdp", axis=0, tiled=True),
        lax.all_gather(w_out, "fsdp", axis=0, tiled=True),
        lax.all_gather(b_out, "fsdp", axis=0, tiled=True),
        lax.all_gather(gain_one, "fsdp", axis=0, tiled=True),
        lax.all_gather(shift_one, "fsdp", axis=0, tiled=True),
        lax.all_gather(w_up, "fsdp", axis=0, tiled=True),
        lax.all_gather(b_up, "fsdp", axis=0, tiled=True),
        lax.all_gather(w_down, "fsdp", axis=0, tiled=True),
        lax.all_gather(b_down, "fsdp", axis=0, tiled=True),
        lax.all_gather(gain_two, "fsdp", axis=0, tiled=True),
        lax.all_gather(shift_two, "fsdp", axis=0, tiled=True),
    )
    seq_count, blk_rows, model_width = tokens.shape
    head_count = model_width // HEAD
    row_count = seq_count * blk_rows
    score_scale = HEAD ** (-0.5)
    ctx_size = lax.axis_size("ctx")
    ctx_place = lax.axis_index("ctx")
    flat_rows = tokens.reshape(row_count, model_width)
    qv_bias = wide_bqv.astype(jnp.float32)
    mixed = jnp.dot(flat_rows, wide_qkv, preferred_element_type=jnp.float32)
    head_shape = (seq_count, blk_rows, head_count, HEAD)
    queries = (
        (mixed[:, :model_width] + qv_bias[:model_width]).astype(jnp.bfloat16).reshape(head_shape)
    )
    keys_low = mixed[:, model_width : 2 * model_width].astype(jnp.bfloat16).reshape(head_shape)
    values_low = (
        (mixed[:, 2 * model_width :] + qv_bias[model_width:])
        .astype(jnp.bfloat16)
        .reshape(head_shape)
    )
    stat_shape = (seq_count, head_count, blk_rows)
    running_max = jnp.full(stat_shape, -1e30, jnp.float32)
    key_piece = lax.all_gather(keys_low, "ctx", axis=1, tiled=True)
    value_piece = lax.all_gather(values_low, "ctx", axis=1, tiled=True)
    scores = (
        jnp.einsum("sqhd,skhd->shqk", queries, key_piece, preferred_element_type=jnp.float32)
        * score_scale
    )
    scores = jnp.where(key_valid(lengths, jnp.int32(0), key_piece.shape[1]), scores, -1e30)
    new_max = jnp.maximum(running_max, jnp.max(scores, axis=-1))
    weights = jnp.exp(scores - new_max[..., None])
    running_sum = jnp.sum(weights, axis=-1)
    running_acc = jnp.einsum(
        "shqk,skhd->shqd",
        weights.astype(jnp.bfloat16),
        value_piece,
        preferred_element_type=jnp.float32,
    )
    log_sums = new_max + jnp.log(running_sum)
    attended_heads = jnp.transpose(running_acc / running_sum[..., None], (0, 2, 1, 3))
    attended = attended_heads.reshape(row_count, model_width)
    attended_low = attended.astype(jnp.bfloat16)
    first_sum = (
        flat_rows.astype(jnp.float32)
        + jnp.dot(attended_low, wide_out, preferred_element_type=jnp.float32)
        + wide_bout.astype(jnp.float32)
    )
    gain_first = wide_gone.astype(jnp.float32)
    normed, hat_first, inv_first = norm_forward(
        first_sum, gain_first, wide_sone.astype(jnp.float32)
    )
    normed_low = normed.astype(jnp.bfloat16)
    hidden = jnp.dot(normed_low, wide_up, preferred_element_type=jnp.float32) + wide_bup.astype(
        jnp.float32
    )
    activated = gelu_exact(hidden).astype(jnp.bfloat16)
    second_sum = (
        normed
        + jnp.dot(activated, wide_down, preferred_element_type=jnp.float32)
        + wide_bdown.astype(jnp.float32)
    )
    gain_second = wide_gtwo.astype(jnp.float32)
    result, hat_second, inv_second = norm_forward(
        second_sum, gain_second, wide_stwo.astype(jnp.float32)
    )
    layer_out = result.astype(jnp.bfloat16).reshape(seq_count, blk_rows, model_width)
    grad_output = cotangent.reshape(row_count, model_width).astype(jnp.float32)
    grad_gtwo = jnp.sum(grad_output * hat_second, axis=0)
    grad_stwo = jnp.sum(grad_output, axis=0)
    d_second = norm_backward(grad_output, hat_second, inv_second, gain_second)
    d_out_low = d_second.astype(jnp.bfloat16)
    grad_wdown = jnp.einsum("ra,rb->ab", activated, d_out_low, preferred_element_type=jnp.float32)
    grad_bdown = jnp.sum(d_out_low, axis=0, dtype=jnp.float32)
    d_activated = jnp.einsum("rb,ab->ra", d_out_low, wide_down, preferred_element_type=jnp.float32)
    d_hidden = (d_activated * gelu_slope(hidden)).astype(jnp.bfloat16)
    grad_wup = jnp.einsum("ra,rb->ab", normed_low, d_hidden, preferred_element_type=jnp.float32)
    grad_bup = jnp.sum(d_hidden, axis=0, dtype=jnp.float32)
    d_normed = d_second + jnp.einsum(
        "rf,df->rd", d_hidden, wide_up, preferred_element_type=jnp.float32
    )
    grad_gone = jnp.sum(d_normed * hat_first, axis=0)
    grad_sone = jnp.sum(d_normed, axis=0)
    d_first = norm_backward(d_normed, hat_first, inv_first, gain_first)
    d_branch = d_first.astype(jnp.bfloat16)
    grad_wout = jnp.einsum("ra,rb->ab", attended_low, d_branch, preferred_element_type=jnp.float32)
    grad_bout = jnp.sum(d_branch, axis=0, dtype=jnp.float32)
    d_attended = jnp.einsum(
        "rb,ab->ra", d_branch, wide_out, preferred_element_type=jnp.float32
    ).astype(jnp.bfloat16)
    d_att_heads = d_attended.reshape(head_shape)
    delta_rows = jnp.einsum("sqhd,sqhd->shq", d_att_heads.astype(jnp.float32), attended_heads)
    zero_heads = jnp.zeros(head_shape, jnp.float32)

    def cycle_turn(turn_index, state_in):
        key_piece, value_piece, grad_keys, grad_values, grad_queries = state_in
        source = (ctx_place - turn_index) % ctx_size
        query_term, key_term, value_term = block_terms(
            queries,
            d_att_heads,
            log_sums,
            delta_rows,
            key_piece,
            value_piece,
            lengths,
            source * blk_rows,
        )
        key_piece, value_piece = shifted((key_piece, value_piece), "ctx", 1)
        grad_keys, grad_values = (
            shifted((grad_keys + key_term).astype(jnp.bfloat16), "ctx", 1).astype(jnp.float32),
            shifted((grad_values + value_term).astype(jnp.bfloat16), "ctx", 1).astype(jnp.float32),
        )
        return (key_piece, value_piece, grad_keys, grad_values, grad_queries + query_term)

    cycle_end = lax.fori_loop(
        0, ctx_size, cycle_turn, (keys_low, values_low, zero_heads, zero_heads, zero_heads)
    )
    grad_keys, grad_values, grad_queries = (cycle_end[2], cycle_end[3], cycle_end[4])
    d_mixed = jnp.concatenate(
        [
            grad_queries.reshape(row_count, model_width),
            grad_keys.reshape(row_count, model_width),
            grad_values.reshape(row_count, model_width),
        ],
        axis=1,
    ).astype(jnp.bfloat16)
    grad_wqkv = jnp.einsum("ra,rb->ab", flat_rows, d_mixed, preferred_element_type=jnp.float32)
    grad_bqv = jnp.concatenate(
        [
            jnp.sum(d_mixed[:, :model_width], axis=0, dtype=jnp.float32),
            jnp.sum(d_mixed[:, 2 * model_width :], axis=0, dtype=jnp.float32),
        ]
    )
    grad_tokens = d_first + jnp.einsum(
        "rc,dc->rd", d_mixed, wide_qkv, preferred_element_type=jnp.float32
    )
    grad_tokens = grad_tokens.reshape(seq_count, blk_rows, model_width)
    all_grads = (
        grad_wqkv,
        grad_bqv,
        grad_wout,
        grad_bout,
        grad_gone,
        grad_sone,
        grad_wup,
        grad_bup,
        grad_wdown,
        grad_bdown,
        grad_gtwo,
        grad_stwo,
    )
    partial_shares = (
        lax.psum_scatter(
            all_grads[0].astype(jnp.bfloat16), "fsdp", scatter_dimension=0, tiled=True
        ).astype(jnp.float32),
        lax.psum_scatter(
            all_grads[1].astype(jnp.bfloat16), "fsdp", scatter_dimension=0, tiled=True
        ).astype(jnp.float32),
        lax.psum_scatter(
            all_grads[2].astype(jnp.bfloat16), "fsdp", scatter_dimension=0, tiled=True
        ).astype(jnp.float32),
        lax.psum_scatter(
            all_grads[3].astype(jnp.bfloat16), "fsdp", scatter_dimension=0, tiled=True
        ).astype(jnp.float32),
        lax.psum_scatter(
            all_grads[4].astype(jnp.bfloat16), "fsdp", scatter_dimension=0, tiled=True
        ).astype(jnp.float32),
        lax.psum_scatter(
            all_grads[5].astype(jnp.bfloat16), "fsdp", scatter_dimension=0, tiled=True
        ).astype(jnp.float32),
        lax.psum_scatter(
            all_grads[6].astype(jnp.bfloat16), "fsdp", scatter_dimension=0, tiled=True
        ).astype(jnp.float32),
        lax.psum_scatter(
            all_grads[7].astype(jnp.bfloat16), "fsdp", scatter_dimension=0, tiled=True
        ).astype(jnp.float32),
        lax.psum_scatter(
            all_grads[8].astype(jnp.bfloat16), "fsdp", scatter_dimension=0, tiled=True
        ).astype(jnp.float32),
        lax.psum_scatter(
            all_grads[9].astype(jnp.bfloat16), "fsdp", scatter_dimension=0, tiled=True
        ).astype(jnp.float32),
        lax.psum_scatter(
            all_grads[10].astype(jnp.bfloat16), "fsdp", scatter_dimension=0, tiled=True
        ).astype(jnp.float32),
        lax.psum_scatter(
            all_grads[11].astype(jnp.bfloat16), "fsdp", scatter_dimension=0, tiled=True
        ).astype(jnp.float32),
    )
    shares = (
        lax.psum_scatter(
            partial_shares[0].astype(jnp.bfloat16), "ctx", scatter_dimension=0, tiled=True
        ).astype(jnp.float32),
        lax.psum_scatter(
            partial_shares[1].astype(jnp.bfloat16), "ctx", scatter_dimension=0, tiled=True
        ).astype(jnp.float32),
        lax.psum_scatter(
            partial_shares[2].astype(jnp.bfloat16), "ctx", scatter_dimension=0, tiled=True
        ).astype(jnp.float32),
        lax.psum_scatter(
            partial_shares[3].astype(jnp.bfloat16), "ctx", scatter_dimension=0, tiled=True
        ).astype(jnp.float32),
        lax.psum_scatter(
            partial_shares[4].astype(jnp.bfloat16), "ctx", scatter_dimension=0, tiled=True
        ).astype(jnp.float32),
        lax.psum_scatter(
            partial_shares[5].astype(jnp.bfloat16), "ctx", scatter_dimension=0, tiled=True
        ).astype(jnp.float32),
        lax.psum_scatter(
            partial_shares[6].astype(jnp.bfloat16), "ctx", scatter_dimension=0, tiled=True
        ).astype(jnp.float32),
        lax.psum_scatter(
            partial_shares[7].astype(jnp.bfloat16), "ctx", scatter_dimension=0, tiled=True
        ).astype(jnp.float32),
        lax.psum_scatter(
            partial_shares[8].astype(jnp.bfloat16), "ctx", scatter_dimension=0, tiled=True
        ).astype(jnp.float32),
        lax.psum_scatter(
            partial_shares[9].astype(jnp.bfloat16), "ctx", scatter_dimension=0, tiled=True
        ).astype(jnp.float32),
        lax.psum_scatter(
            partial_shares[10].astype(jnp.bfloat16), "ctx", scatter_dimension=0, tiled=True
        ).astype(jnp.float32),
        lax.psum_scatter(
            partial_shares[11].astype(jnp.bfloat16), "ctx", scatter_dimension=0, tiled=True
        ).astype(jnp.float32),
    )
    return (
        layer_out,
        grad_tokens,
        shares[0],
        shares[1],
        shares[2],
        shares[3],
        shares[4],
        shares[5],
        shares[6],
        shares[7],
        shares[8],
        shares[9],
        shares[10],
        shares[11],
    )


def swap_core(value):
    length = lax.axis_size("ctx")
    return lax.ppermute(value, "ctx", [(i, i ^ 1) for i in range(length)])


def hop(value, bit):
    return lax.ppermute(value, "fsdp", [(i, i ^ bit) for i in range(4)])


def take(value, place, axis=0):
    return lax.dynamic_index_in_dim(value, place, axis, keepdims=False)


def after(value, *others):
    return lax.optimization_barrier((value,) + others)[0]


def sum_everywhere(value):
    for bit in (1, 2, 4):
        length = lax.axis_size("ctx")
        value = value + lax.ppermute(value, "ctx", [(i, i ^ bit) for i in range(length)])
    for bit in (1, 2):
        value = value + hop(value, bit)
    return value


def gather_vector(value):
    place = lax.axis_index("fsdp")
    one, two = hop(value, 1), hop(value, 2)
    near = jnp.stack([value, one, two, hop(one, 2)])
    return jnp.stack([take(near, place ^ i) for i in range(4)])


def gather_weight(shard):
    place, core = lax.axis_index("fsdp"), lax.axis_index("ctx") % 2
    rows = shard.shape[0]
    half, quarter = rows // 2, rows // 4
    own = lax.dynamic_slice_in_dim(shard, core * half, half, 0)
    from_x, from_y = hop(own, 1), hop(own, 2)
    far = jnp.concatenate([hop(from_x[:quarter], 2), hop(from_y[quarter:], 1)], axis=0)
    whole = jnp.zeros((4 * rows,) + shard.shape[1:], shard.dtype)
    whole = lax.dynamic_update_slice_in_dim(whole, shard, place * rows, 0)
    for bit, piece in ((1, from_x), (2, from_y), (3, far)):
        start = (place ^ bit) * rows
        whole = lax.dynamic_update_slice_in_dim(whole, piece, start + core * half, 0)
        whole = lax.dynamic_update_slice_in_dim(
            whole, swap_core(piece), start + (1 - core) * half, 0
        )
    return whole, far


def pair_sum(left, right):
    core = lax.axis_index("ctx") % 2
    rows, width = left.shape
    share = width // (4 * lax.axis_size("ctx"))
    split = left.reshape(rows, width // (2 * share), 2, share)

    def product(which):
        part = take(split, which, 2).reshape(rows, width // 2)
        return jnp.einsum("ra,rb->ab", part, right, preferred_element_type=jnp.float32)

    given = swap_core(product(1 - core).astype(jnp.bfloat16))
    sums = (product(core) + given.astype(jnp.float32)).astype(jnp.bfloat16)
    return sums.reshape(4, width // 8, right.shape[1])


def pass_far(sums):
    far = take(sums, lax.axis_index("fsdp") ^ 3)
    half = far.shape[0] // 2
    return hop(far[:half], 1), hop(far[half:], 2)


def pass_near(sums, passed):
    place = lax.axis_index("fsdp")
    pass_y, pass_x = passed
    half = pass_y.shape[0]
    for_x, for_y = take(sums, place ^ 1), take(sums, place ^ 2)
    got_x = hop(jnp.concatenate([for_x[:half], for_x[half:] + pass_x], axis=0), 1)
    got_y = hop(jnp.concatenate([for_y[:half] + pass_y, for_y[half:]], axis=0), 2)
    return (
        take(sums, place).astype(jnp.float32)
        + got_x.astype(jnp.float32)
        + got_y.astype(jnp.float32)
    ).astype(jnp.bfloat16)


def scatter_chips(mine):
    groups = [[2 * i + c for i in range(lax.axis_size("ctx") // 2)] for c in range(2)]
    return lax.psum_scatter(
        mine, "ctx", scatter_dimension=0, tiled=True, axis_index_groups=groups
    ).astype(jnp.float32)


def exchange(value):
    return lax.all_to_all(value, "ctx", split_axis=0, concat_axis=0, tiled=True)


def dot_rows(left, right):
    return lax.dot_general(
        left, right, (((1,), (1,)), ((), ())), preferred_element_type=jnp.float32
    )


def head_probs(query, key, valid):
    scores = jnp.where(valid, dot_rows(query, key) * (HEAD ** (-0.5)), -1e30)
    weights = jnp.exp(scores - jnp.max(scores, axis=1, keepdims=True))
    return weights, jnp.sum(weights, axis=1, keepdims=True)


def merged(ref):
    value = ref[...]
    return value.reshape(value.shape[0] * value.shape[2], value.shape[3])


def attend_kernel(lengths_ref, query_ref, key_ref, value_ref, out_ref):
    query, key, value = merged(query_ref), merged(key_ref), merged(value_ref)
    rows, keys = query.shape[0], key.shape[0]
    valid = lax.broadcasted_iota(jnp.int32, (rows, keys), 1) < lengths_ref[pl.program_id(0)]
    lower = lax.broadcasted_iota(jnp.int32, (rows, GROUP), 1) < HEAD
    outs = []
    for head in range(2):
        picked = jnp.where(lower == (head == 0), query, jnp.zeros_like(query))
        weights, total = head_probs(picked, key, valid)
        acc = jnp.dot(weights.astype(jnp.bfloat16), value, preferred_element_type=jnp.float32)
        outs.append(acc / total)
    out = jnp.where(lower, outs[0], outs[1]).astype(jnp.bfloat16)
    out_ref[...] = out.reshape(out_ref.shape)


def attend_back_kernel(
    lengths_ref, query_ref, key_ref, value_ref, grad_ref, out_ref, key_acc, value_acc
):
    step = pl.program_id(1)
    query, key, value, grad = (
        merged(query_ref),
        merged(key_ref),
        merged(value_ref),
        merged(grad_ref),
    )
    rows, keys = query.shape[0], key.shape[0]
    blocks = query_ref.shape[0]
    valid = lax.broadcasted_iota(jnp.int32, (rows, keys), 1) < lengths_ref[pl.program_id(0)]
    lower = lax.broadcasted_iota(jnp.int32, (rows, GROUP), 1) < HEAD

    @pl.when(step == 0)
    def _():
        key_acc[...] = jnp.zeros_like(key_acc)
        value_acc[...] = jnp.zeros_like(value_acc)

    grads = []
    for head in range(2):
        mine = lower == (head == 0)
        picked = jnp.where(mine, query, jnp.zeros_like(query))
        picked_grad = jnp.where(mine, grad, jnp.zeros_like(grad))
        weights, total = head_probs(picked, key, valid)
        probs = weights / total
        d_probs = dot_rows(picked_grad, value)
        delta = jnp.sum(probs * d_probs, axis=1, keepdims=True)
        d_scores = (probs * (d_probs - delta)).astype(jnp.bfloat16)
        over_rows = (((0,), (0,)), ((), ()))
        value_acc[...] += lax.dot_general(
            probs.astype(jnp.bfloat16), picked_grad, over_rows, preferred_element_type=jnp.float32
        )
        key_acc[...] += lax.dot_general(
            d_scores, picked, over_rows, preferred_element_type=jnp.float32
        )
        grads.append(jnp.dot(d_scores, key, preferred_element_type=jnp.float32))
    d_query = jnp.where(lower, grads[0], grads[1]) * (HEAD ** (-0.5))
    out_ref[pl.ds(step * blocks, blocks), :, :, 0:GROUP] = d_query.astype(jnp.bfloat16).reshape(
        query_ref.shape
    )

    @pl.when(step == pl.num_programs(1) - 1)
    def _():
        shape = key_ref.shape
        d_key = (key_acc[...] * (HEAD ** (-0.5))).astype(jnp.bfloat16)
        out_ref[:, :, :, GROUP : 2 * GROUP] = d_key.reshape(shape)
        out_ref[:, :, :, 2 * GROUP : 3 * GROUP] = value_acc[...].astype(jnp.bfloat16).reshape(shape)


def attend_specs(parts, blk_rows, blocks):
    def query_part(s, i):
        return (i, s, 0, 0)

    def whole_part(which):
        return pl.BlockSpec((parts, 1, blk_rows, GROUP), lambda s, i: (0, s, 0, which))

    query_spec = pl.BlockSpec((blocks, 1, blk_rows, GROUP), query_part)
    return query_spec, whole_part(1), whole_part(2)


def attend(lengths, packed, blocks=2):
    parts, seq_count, blk_rows, _ = packed.shape
    query_spec, key_spec, value_spec = attend_specs(parts, blk_rows, blocks)
    return pl.pallas_call(
        attend_kernel,
        grid=(seq_count, parts // blocks),
        in_specs=[pl.BlockSpec(memory_space=pltpu.SMEM), query_spec, key_spec, value_spec],
        out_specs=query_spec,
        out_shape=jax.ShapeDtypeStruct((parts, seq_count, blk_rows, GROUP), jnp.bfloat16),
        compiler_params=pltpu.CompilerParams(vmem_limit_bytes=VMEM_BYTES),
        cost_estimate=pl.CostEstimate(
            flops=8 * GROUP * seq_count * (parts * blk_rows) ** 2,
            bytes_accessed=8 * seq_count * parts * blk_rows * GROUP,
            transcendentals=2 * seq_count * (parts * blk_rows) ** 2,
        ),
    )(lengths, packed, packed, packed)


def attend_back(lengths, packed, grad, blocks=2):
    parts, seq_count, blk_rows, width = packed.shape
    query_spec, key_spec, value_spec = attend_specs(parts, blk_rows, blocks)
    return pl.pallas_call(
        attend_back_kernel,
        grid=(seq_count, parts // blocks),
        in_specs=[
            pl.BlockSpec(memory_space=pltpu.SMEM),
            query_spec,
            key_spec,
            value_spec,
            query_spec,
        ],
        out_specs=pl.BlockSpec((parts, 1, blk_rows, width), lambda s, i: (0, s, 0, 0)),
        out_shape=jax.ShapeDtypeStruct(packed.shape, jnp.bfloat16),
        scratch_shapes=[pltpu.VMEM((parts * blk_rows, GROUP), jnp.float32)] * 2,
        compiler_params=pltpu.CompilerParams(vmem_limit_bytes=VMEM_BYTES),
        cost_estimate=pl.CostEstimate(
            flops=20 * GROUP * seq_count * (parts * blk_rows) ** 2,
            bytes_accessed=16 * seq_count * parts * blk_rows * GROUP,
            transcendentals=2 * seq_count * (parts * blk_rows) ** 2,
        ),
    )(lengths, packed, packed, packed, grad)


def local_heads(
    tokens,
    lengths,
    w_qkv,
    b_qv,
    w_out,
    b_out,
    gain_one,
    shift_one,
    w_up,
    b_up,
    w_down,
    b_down,
    gain_two,
    shift_two,
    cotangent,
):
    ctx_size = lax.axis_size("ctx")
    place, ctx_place = lax.axis_index("fsdp"), lax.axis_index("ctx")
    seq_count, blk_rows, model_width = tokens.shape
    row_count = seq_count * blk_rows
    wide_qkv, far_qkv = gather_weight(w_qkv)
    vectors = (b_qv, b_out, gain_one, shift_one, b_up, b_down, gain_two, shift_two)
    joined = gather_vector(jnp.concatenate(vectors))
    wide, start = [], 0
    for vector in vectors:
        stop = start + vector.shape[0]
        wide.append(joined[:, start:stop].reshape(-1).astype(jnp.float32))
        start = stop
    qv_bias, out_bias, gain_first, shift_first, up_bias, down_bias, gain_second, shift_second = wide
    wide_out, far_out = gather_weight(after(w_out, far_qkv))
    wide_up, far_up = gather_weight(after(w_up, far_out))
    wide_down, _ = gather_weight(after(w_down, far_up))
    flat_rows = tokens.reshape(row_count, model_width)
    mixed = jnp.dot(flat_rows, wide_qkv, preferred_element_type=jnp.float32)
    mixed_bias = jnp.concatenate(
        [qv_bias[:model_width], jnp.zeros((model_width,), jnp.float32), qv_bias[model_width:]]
    )
    mixed_low = (mixed + mixed_bias).astype(jnp.bfloat16)
    packed = jnp.transpose(
        mixed_low.reshape(seq_count, blk_rows, 3, ctx_size, GROUP), (3, 0, 1, 2, 4)
    ).reshape(ctx_size, seq_count, blk_rows, 3 * GROUP)
    packed = exchange(packed)
    attended_low = jnp.transpose(exchange(attend(lengths, packed)), (1, 2, 0, 3)).reshape(
        row_count, model_width
    )
    first_sum = (
        flat_rows.astype(jnp.float32)
        + jnp.dot(attended_low, wide_out, preferred_element_type=jnp.float32)
        + out_bias
    )
    normed, hat_first, inv_first = norm_forward(first_sum, gain_first, shift_first)
    normed_low = normed.astype(jnp.bfloat16)
    hidden = jnp.dot(normed_low, wide_up, preferred_element_type=jnp.float32) + up_bias
    activated = gelu_exact(hidden).astype(jnp.bfloat16)
    second_sum = (
        normed + jnp.dot(activated, wide_down, preferred_element_type=jnp.float32) + down_bias
    )
    result, hat_second, inv_second = norm_forward(second_sum, gain_second, shift_second)
    layer_out = result.astype(jnp.bfloat16).reshape(seq_count, blk_rows, model_width)
    grad_output = cotangent.reshape(row_count, model_width).astype(jnp.float32)
    grad_gtwo = jnp.sum(grad_output * hat_second, axis=0)
    grad_stwo = jnp.sum(grad_output, axis=0)
    d_second = norm_backward(grad_output, hat_second, inv_second, gain_second)
    d_out_low = d_second.astype(jnp.bfloat16)
    sums_down = pair_sum(activated, d_out_low)
    grad_bdown = jnp.sum(d_out_low, axis=0, dtype=jnp.float32)
    d_activated = jnp.einsum("rb,ab->ra", d_out_low, wide_down, preferred_element_type=jnp.float32)
    d_hidden = (d_activated * gelu_slope(hidden)).astype(jnp.bfloat16)
    sums_up = pair_sum(normed_low, d_hidden)
    grad_bup = jnp.sum(d_hidden, axis=0, dtype=jnp.float32)
    d_normed = d_second + jnp.einsum(
        "rf,df->rd", d_hidden, wide_up, preferred_element_type=jnp.float32
    )
    grad_gone = jnp.sum(d_normed * hat_first, axis=0)
    grad_sone = jnp.sum(d_normed, axis=0)
    d_first = norm_backward(d_normed, hat_first, inv_first, gain_first)
    d_branch = d_first.astype(jnp.bfloat16)
    sums_out = pair_sum(attended_low, d_branch)
    grad_bout = jnp.sum(d_branch, axis=0, dtype=jnp.float32)
    d_attended = jnp.einsum(
        "rb,ab->ra", d_branch, wide_out, preferred_element_type=jnp.float32
    ).astype(jnp.bfloat16)
    d_packed = jnp.transpose(
        d_attended.reshape(seq_count, blk_rows, ctx_size, GROUP), (2, 0, 1, 3)
    )
    d_packed = after(d_packed, sums_down, sums_up)
    far_down = pass_far(sums_down)
    d_packed = after(exchange(d_packed), *far_down)
    mine_down = pass_near(sums_down, far_down)
    far_up = pass_far(after(sums_up, far_down[0]))
    d_parts = after(attend_back(lengths, packed, d_packed), mine_down, *far_up)
    share_down = scatter_chips(mine_down)
    mine_up = pass_near(sums_up, far_up)
    far_out = pass_far(sums_out)
    d_parts = after(exchange(d_parts), mine_up, *far_out)
    share_up = scatter_chips(mine_up)
    d_mixed = jnp.transpose(
        d_parts.reshape(ctx_size, seq_count, blk_rows, 3, GROUP), (1, 2, 3, 0, 4)
    ).reshape(row_count, 3 * model_width)
    sums_qkv = pair_sum(flat_rows, d_mixed)
    share_out = scatter_chips(pass_near(sums_out, far_out))
    share_qkv = scatter_chips(pass_near(sums_qkv, pass_far(sums_qkv)))
    grad_bqv = jnp.concatenate(
        [
            jnp.sum(d_mixed[:, :model_width], axis=0, dtype=jnp.float32),
            jnp.sum(d_mixed[:, 2 * model_width :], axis=0, dtype=jnp.float32),
        ]
    )
    grad_tokens = d_first + jnp.einsum(
        "rc,dc->rd", d_mixed, wide_qkv, preferred_element_type=jnp.float32
    )
    grad_tokens = grad_tokens.reshape(seq_count, blk_rows, model_width)
    small = (
        grad_bqv,
        grad_bout,
        grad_gone,
        grad_sone,
        grad_bup,
        grad_bdown,
        grad_gtwo,
        grad_stwo,
    )
    device_count = 4 * ctx_size
    joined = jnp.concatenate([item.reshape(device_count, -1) for item in small[1:]], axis=1)
    joined = jnp.concatenate(
        [sum_everywhere(small[0].reshape(device_count, -1)), sum_everywhere(joined)], axis=1
    )
    joined = take(joined, place * ctx_size + ctx_place)
    shares, start = [], 0
    for item in small:
        stop = start + item.shape[0] // device_count
        shares.append(joined[start:stop])
        start = stop
    return (
        layer_out,
        grad_tokens,
        share_qkv,
        shares[0],
        share_out,
        shares[1],
        shares[2],
        shares[3],
        share_up,
        shares[4],
        share_down,
        shares[5],
        shares[6],
        shares[7],
    )


def solution(mesh):
    by_heads = mesh.shape["fsdp"] == 4 and mesh.shape["ctx"] == 8
    return jax.shard_map(
        local_heads if by_heads else local,
        mesh=mesh,
        in_specs=(
            P("fsdp", "ctx", None),
            P("fsdp"),
            P("fsdp", None),
            P("fsdp"),
            P("fsdp", None),
            P("fsdp"),
            P("fsdp"),
            P("fsdp"),
            P("fsdp", None),
            P("fsdp"),
            P("fsdp", None),
            P("fsdp"),
            P("fsdp"),
            P("fsdp"),
            P("fsdp", "ctx", None),
        ),
        out_specs=(
            P("fsdp", "ctx", None),
            P("fsdp", "ctx", None),
            P(("fsdp", "ctx"), None),
            P(("fsdp", "ctx")),
            P(("fsdp", "ctx"), None),
            P(("fsdp", "ctx")),
            P(("fsdp", "ctx")),
            P(("fsdp", "ctx")),
            P(("fsdp", "ctx"), None),
            P(("fsdp", "ctx")),
            P(("fsdp", "ctx"), None),
            P(("fsdp", "ctx")),
            P(("fsdp", "ctx")),
            P(("fsdp", "ctx")),
        ),
        check_vma=False,
    )
```
